256 devices in a mesh: wide: 32 (over z, y_lo, core), narrow: 8 (over y_hi, x).
Axes of the slice: x: 4, y: 4 (y_hi: 2, y_lo: 2; y = y_hi * 2 + y_lo), z: 8, core: 2. Of those that a mesh axis runs over, the one named last changes fastest.
Arguments:
- tokens: bfloat16 [64, 2048, 3072], P('wide', 'narrow'), may hold values from -6 to 6
- gain: float32 [3072], replicated, may hold values from 0.25 to 1.75
- w_qkv: bfloat16 [3072, 4608], P(None, 'narrow'), may hold values from -2 to 2
- band: int32 [12], replicated, may hold values from 8 to 63
Outputs:
- attended: bfloat16 [64, 2048, 1536], P('wide', 'narrow')
The draws below stay inside these ranges and needn't reach their ends.
Inputs may be any that keep to these rules, and one draw needn't show every extreme that they name: A key frame u is used for query frame t in head h when |t - u| <= band[h].
All inputs are finite; a program needn't handle non-finite values.
Results may differ from the reference program's by a relative error of at most 0.0082.
Values may be sent and summed in bfloat16 or wider, within the bound.
No kernel may reach another device: no remote copies, remote signals or barrier semaphores. Data moves between devices by JAX's collectives and lax.ppermute only.
A program may use at most 128 MiB of HBM per device.

```python
import math
import jax
import jax.numpy as jnp
from jax import lax

D = 3072
HEADS = 12
HD = 128
FRAMES = 64
INNER = 1536
S = 2048


def draw_tokens(key, part):
    key = jax.random.fold_in(key, 11)
    values = jax.random.normal(key, (FRAMES, S, D), jnp.float32)
    return jnp.clip(values, -6.0, 6.0).astype(jnp.bfloat16)


def draw_w_qkv(key, part):
    key = jax.random.fold_in(key, 23)
    values = jax.random.normal(key, (D, 3 * INNER), jnp.float32) * D ** (-0.5)
    return jnp.clip(values, -2.0, 2.0).astype(jnp.bfloat16)


def with_ends(values, key, least, largest):
    longest = values.shape.index(max(values.shape))
    spots = []
    for shift in (0, 1):
        where = [jax.random.randint(jax.random.fold_in(key, axis), (), 0, length) for axis, length in enumerate(values.shape)]
        where[longest] = (where[longest] + shift) % values.shape[longest]
        spots.append(tuple(where))
    return values.at[spots[0]].set(least).at[spots[1]].set(largest)


def setup_inputs(seed: int = 0) -> dict:
    streams_of = jax.random.split(jax.random.key(seed), 5)
    tokens = draw_tokens(jax.random.fold_in(streams_of[4], 71), 0)
    gain = jnp.clip(1.0 + 0.15 * jax.random.normal(streams_of[1], (D,), jnp.float32), 0.25, 1.75)
    w_qkv = draw_w_qkv(jax.random.fold_in(streams_of[4], 71), 0)
    band = with_ends(jax.random.randint(streams_of[3], (HEADS,), FRAMES // 8, FRAMES), jax.random.fold_in(streams_of[3], 1), FRAMES // 8, FRAMES - 1).astype(jnp.int32)
    return dict(tokens=tokens, gain=gain, w_qkv=w_qkv, band=band)


EPS = 1e-06

def normalize(tokens, gain):
    values = tokens.astype(jnp.float32)
    centered = values - lax.optimization_barrier(jnp.mean(values, axis=-1, keepdims=True))
    spread = lax.optimization_barrier(jnp.mean(centered * centered, axis=-1, keepdims=True))
    return (centered * lax.rsqrt(spread + EPS) * gain).astype(jnp.bfloat16)

def temporal(qkv, band):
    frames, count = (qkv.shape[0], qkv.shape[1])
    query = qkv[..., :INNER].reshape(frames, count, HEADS, HD).astype(jnp.float32)
    keys = qkv[..., INNER:2 * INNER].reshape(frames, count, HEADS, HD).astype(jnp.float32)
    values = qkv[..., 2 * INNER:].reshape(frames, count, HEADS, HD).astype(jnp.float32)
    scores = jnp.einsum('tbhe,ubhe->bhtu', query, keys) * (1.0 / math.sqrt(HD))
    steps_t = jnp.arange(frames, dtype=jnp.int32)
    distance = jnp.abs(steps_t[:, None] - steps_t[None, :])
    allowed = distance[None, None, :, :] <= band[None, :, None, None]
    scores = jnp.where(allowed, scores, -jnp.inf)
    highest = lax.optimization_barrier(jnp.max(scores, axis=-1, keepdims=True))
    weights = jnp.exp(scores - highest)
    total = lax.optimization_barrier(jnp.sum(weights, axis=-1, keepdims=True))
    probs = (weights / total).astype(jnp.bfloat16)
    result = jnp.einsum('bhtu,ubhe->tbhe', probs.astype(jnp.float32), values)
    return result.astype(jnp.bfloat16).reshape(frames, count, INNER)

def reference(tokens, gain, w_qkv, band):
    block = math.gcd(S, 64)
    count = S // block

    def one_block(index):
        piece = lax.dynamic_slice_in_dim(tokens, index * block, block, 1)
        normed = normalize(piece, gain)
        qkv = jnp.dot(normed.reshape(-1, D), w_qkv, preferred_element_type=jnp.float32)
        qkv = qkv.astype(jnp.bfloat16).reshape(FRAMES, block, 3 * INNER)
        return temporal(qkv, band)
    blocks = lax.map(one_block, jnp.arange(count, dtype=jnp.int32))
    return jnp.transpose(blocks, (1, 0, 2, 3)).reshape(FRAMES, S, INNER)
```

```python
import math

import jax
import jax.numpy as jnp
from jax import lax
from jax.experimental import pallas as pl
from jax.experimental.pallas import tpu as pltpu
from jax.sharding import Mesh, PartitionSpec as P

HD = 128
INNER = 1536
WIDTH = 3072
HALF = 1536
EPS = 1e-06
SIZES = (8, 2, 2, 2, 4)
NAMES = ("z", "yl", "c", "yh", "x")
WIDE = ("z", "yl", "c")
GROUPS = ((0,), (1, 7), (2, 6), (3, 5), (4,))


def normalize(tokens, gain):
    values = tokens.astype(jnp.float32)
    centered = values - jnp.mean(values, axis=-1, keepdims=True)
    spread = jnp.mean(centered * centered, axis=-1, keepdims=True)
    return (centered * lax.rsqrt(spread + EPS) * gain).astype(jnp.bfloat16)


def send(value, move):
    pairs = []
    for i in range(256):
        z, yl, c, yh, x = i // 32, i // 16 % 2, i // 8 % 2, i // 4 % 2, i % 4
        z, yl, c, yh, x = move(z, yl, c, yh, x)
        pairs.append((i, (((z * 2 + yl) * 2 + c) * 2 + yh) * 4 + x))
    return lax.ppermute(value, NAMES, pairs)


def right(v):
    return send(v, lambda z, yl, c, yh, x: (z, yl, c, yh, (x + 1) % 4))


def left(v):
    return send(v, lambda z, yl, c, yh, x: (z, yl, c, yh, (x + 3) % 4))


def outer(v):
    return send(v, lambda z, yl, c, yh, x: (z, 1 - yl, c, 1 - yh, x))


def inner(v):
    return send(v, lambda z, yl, c, yh, x: (z, 1 - yl, c, yh, x))


def other_core(v):
    return send(v, lambda z, yl, c, yh, x: (z, yl, 1 - c, yh, x))


def shifted(v, k):
    return send(v, lambda z, yl, c, yh, x: ((z + k) % 8, yl, c, yh, x))


def after(value, *done):
    return lax.optimization_barrier((value,) + done)[0]


def weights(w, yl, c, yh, x):
    n = yh * 4 + x
    kind = yl ^ yh
    wt = w.T

    def unit(group):
        place = n + (n >= 1 + 2 * group).astype(jnp.int32)
        row = 64 * (2 * (4 * place + group) - 9 * n)
        return lax.dynamic_slice(wt, (row, c * HALF), (128, HALF))

    second = unit(kind + 2)
    extra = lax.dynamic_slice(wt, (512 * (1 - n % 2), c * HALF), (64, HALF))
    own = jnp.concatenate([unit(kind), extra], axis=0)
    members = [
        [(((p ^ b) * 2 + k) * 2 + b) * 4 + a for b in range(2) for a in range(4)] for p in range(2) for k in range(2)
    ]
    whole = lax.all_gather(own, ("yl", "c", "yh", "x"), axis_index_groups=members, axis=0)
    far = outer(second)
    lx, rx = right(second), left(second)
    o0, o1 = right(lx[:64]), left(rx[64:])
    ready = after(far, o0, o1)
    fl, fr = right(ready), left(ready)
    f0, f1 = right(fl[:64]), left(fr[64:])
    near, away = yh * 4, (1 - yh) * 4
    l, r, o = (x + 3) % 4, (x + 1) % 4, (x + 2) % 4
    two = jnp.zeros((8, 128, HALF), jnp.bfloat16)
    for v, at, row in (
        (second, near + x, 0),
        (lx, near + l, 0),
        (rx, near + r, 0),
        (o0, near + o, 0),
        (o1, near + o, 64),
        (far, away + x, 0),
        (fl, away + l, 0),
        (fr, away + r, 0),
        (f0, away + o, 0),
        (f1, away + o, 64),
    ):
        two = lax.dynamic_update_slice(two, v[None], (at, row, 0))

    def pick(core):
        main = jnp.where(core == 0, whole[:, :128], two)
        rest = lax.dynamic_slice(whole, (2 * (kind + 2 * core), 128, 0), (2, 64, HALF)).reshape(1, 128, HALF)
        spot = 1 + 2 * (kind + 2 * core)
        j = jnp.arange(9, dtype=jnp.int32)[:, None, None]
        early = jnp.concatenate([main, rest], axis=0)
        late = jnp.concatenate([rest, main], axis=0)
        return jnp.where(j < spot, early, jnp.where(j == spot, rest, late))

    got = other_core(pick(1 - c)).reshape(1152, HALF)
    mine = pick(c).reshape(1152, HALF)
    return jnp.concatenate([jnp.where(c == 0, mine, got), jnp.where(c == 0, got, mine)], axis=1), far


def attend(qkv, band, frame):
    q, k, v = (qkv[:, 384 * i : 384 * i + 384].reshape(64, 32, 3, HD) for i in range(3))
    scores = jnp.einsum("tbhe,ubhe->bhtu", q, k, preferred_element_type=jnp.float32) * (1.0 / math.sqrt(HD))
    distance = jnp.abs(frame[:, None] - frame[None, :])
    allowed = distance[None, None, :, :] <= band[None, :, None, None]
    scores = jnp.where(allowed, scores, -jnp.inf)
    highest = jnp.max(scores, axis=-1, keepdims=True)
    e = jnp.exp(scores - highest)
    total = jnp.sum(e, axis=-1, keepdims=True)
    probs = (e / total).astype(jnp.bfloat16)
    result = jnp.einsum("bhtu,ubhe->tbhe", probs, v, preferred_element_type=jnp.float32)
    return result.astype(jnp.bfloat16).reshape(32, 64, 384)


def reorder(blocks, order):
    def kernel(order_ref, in_ref, out_ref):
        def body(i, carry):
            out_ref[i] = in_ref[order_ref[i]]
            return carry

        lax.fori_loop(0, 32, body, 0)

    return pl.pallas_call(
        kernel,
        out_shape=jax.ShapeDtypeStruct((32, 64, 384), jnp.bfloat16),
        in_specs=[pl.BlockSpec(memory_space=pltpu.SMEM), pl.BlockSpec(memory_space=pltpu.VMEM)],
        out_specs=pl.BlockSpec(memory_space=pltpu.VMEM),
        compiler_params=pltpu.CompilerParams(vmem_limit_bytes=16 * 2**20),
        name="reorder",
    )(order, blocks)


def spread(blocks, source):
    def kernel(source_ref, in_ref, out_ref):
        def body(z, carry):
            rows = pl.ds(pl.multiple_of(z * 32, 32), 32)
            for g in range(4):
                w = z * 4 + source_ref[g]
                for f in range(2):
                    for i in range(3):
                        column = (4 * i + g) * HD
                        out_ref[f, rows, column : column + HD] = in_ref[w, f * 32 : f * 32 + 32, i * HD : i * HD + HD]
            return carry

        lax.fori_loop(0, 8, body, 0)

    return pl.pallas_call(
        kernel,
        out_shape=jax.ShapeDtypeStruct((2, 256, INNER), jnp.bfloat16),
        in_specs=[pl.BlockSpec(memory_space=pltpu.SMEM), pl.BlockSpec(memory_space=pltpu.VMEM)],
        out_specs=pl.BlockSpec(memory_space=pltpu.VMEM),
        compiler_params=pltpu.CompilerParams(vmem_limit_bytes=16 * 2**20),
        name="spread",
    )(source, blocks)


def per_device(tokens, gain, w_qkv, band):
    z, yl, c, yh, x = (lax.axis_index(n) for n in NAMES)
    w, first = weights(w_qkv, yl, c, yh, x)
    normed = normalize(tokens, gain).reshape(2, 8, 32, WIDTH)

    def block(k):
        to = (z + k) % 8
        return lax.dynamic_slice(normed, (0, to, 0, 0), (2, 1, 32, WIDTH)).reshape(64, WIDTH)

    outs, frames, owners = [], [], []
    came = ()
    for group in GROUPS:
        if group[0] == 0:
            here = after(block(0), first)
        else:
            came = tuple(shifted(after(block(k), *came), k) for k in group)
            here = jnp.concatenate(came, axis=0)
        pair = jnp.concatenate([here, inner(here)], axis=0)
        four = jnp.concatenate([pair, other_core(pair)], axis=0)
        y = lax.dot_general(four, w, (((1,), (1,)), ((), ())), preferred_element_type=jnp.float32)
        outs.append(y.astype(jnp.bfloat16))
        for b in range(2):
            for a in range(2):
                for k in group:
                    owner = ((z - k) % 8) * 4 + (yl ^ a) * 2 + (c ^ b)
                    owners.append(owner)
                    frames += [owner * 2, owner * 2 + 1]
    kind = yl ^ yh
    mine = lax.dynamic_slice(band.reshape(3, 4), (0, kind + 2 * c), (3, 1)).reshape(3)
    result = attend(jnp.concatenate(outs, axis=0), mine, jnp.stack(frames))
    w = jnp.arange(32, dtype=jnp.int32)
    order = jnp.sum(jnp.where(jnp.stack(owners)[None, :] == w[:, None], w[None, :], 0), axis=1)
    back = lax.all_to_all(reorder(result, order), WIDE, 0, 0, tiled=True)
    g = jnp.arange(4, dtype=jnp.int32)
    return spread(back, ((g % 2) ^ yh) * 2 + g // 2)


def solution(mesh):
    own = Mesh(mesh.devices.reshape(SIZES), NAMES)
    tok = P(WIDE, ("yh", "x"), None)
    placed = (tok, P(), P(None, ("yh", "x")), P())
    return jax.shard_map(per_device, mesh=own, in_specs=placed, out_specs=tok, check_vma=False)
```

```python
import math

import jax
import jax.numpy as jnp
from jax import lax
from jax.experimental import pallas as pl
from jax.experimental.pallas import tpu as pltpu
from jax.sharding import Mesh, PartitionSpec as P

HD = 128
INNER = 1536
WIDTH = 3072
HALF = 1536
EPS = 1e-06
SIZES = (8, 2, 2, 2, 4)
NAMES = ("z", "yl", "c", "yh", "x")
WIDE = ("z", "yl", "c")


def normalize(tokens, gain):
    values = tokens.astype(jnp.float32)
    centered = values - jnp.mean(values, axis=-1, keepdims=True)
    spread = jnp.mean(centered * centered, axis=-1, keepdims=True)
    return (centered * lax.rsqrt(spread + EPS) * gain).astype(jnp.bfloat16)


def send(value, move):
    pairs = []
    for i in range(256):
        z, yl, c, yh, x = i // 32, i // 16 % 2, i // 8 % 2, i // 4 % 2, i % 4
        z, yl, c, yh, x = move(z, yl, c, yh, x)
        pairs.append((i, (((z * 2 + yl) * 2 + c) * 2 + yh) * 4 + x))
    return lax.ppermute(value, NAMES, pairs)


def right(v):
    return send(v, lambda z, yl, c, yh, x: (z, yl, c, yh, (x + 1) % 4))


def left(v):
    return send(v, lambda z, yl, c, yh, x: (z, yl, c, yh, (x + 3) % 4))


def outer(v):
    return send(v, lambda z, yl, c, yh, x: (z, 1 - yl, c, 1 - yh, x))


def inner(v):
    return send(v, lambda z, yl, c, yh, x: (z, 1 - yl, c, yh, x))


def other_core(v):
    return send(v, lambda z, yl, c, yh, x: (z, yl, 1 - c, yh, x))


def shifted(v, k):
    return send(v, lambda z, yl, c, yh, x: ((z + k) % 8, yl, c, yh, x))


def after(value, *done):
    return lax.optimization_barrier((value,) + done)[0]


def own_rows(w, c, yh, x, kind):
    n = yh * 4 + x
    wt = w.T

    def unit(group):
        place = n + (n >= 1 + 2 * group).astype(jnp.int32)
        row = 64 * (2 * (4 * place + group) - 9 * n)
        return lax.dynamic_slice(wt, (row, c * HALF), (128, HALF))

    extra = lax.dynamic_slice(wt, (512 * (1 - n % 2), c * HALF), (64, HALF))
    return unit(kind), jnp.concatenate([unit(kind + 2), extra], axis=0)


def gathered(unit):
    members = [
        [(((p ^ b) * 2 + k) * 2 + b) * 4 + a for b in range(2) for a in range(4)] for p in range(2) for k in range(2)
    ]
    return lax.all_gather(unit, ("yl", "c", "yh", "x"), axis_index_groups=members, axis=0)


def pick(units, more, core, kind):
    main = jnp.where(core == 0, units, more[:, :128])
    rest = lax.dynamic_slice(more, (2 * (kind + 2 * core), 128, 0), (2, 64, HALF)).reshape(1, 128, HALF)
    spot = 1 + 2 * (kind + 2 * core)
    j = jnp.arange(9, dtype=jnp.int32)[:, None, None]
    early = jnp.concatenate([main, rest], axis=0)
    late = jnp.concatenate([rest, main], axis=0)
    return jnp.where(j < spot, early, jnp.where(j == spot, rest, late)).reshape(1152, HALF)


def attend(qkv, band, frame):
    q, k, v = (
        jnp.stack([qkv[:, HD * (3 * i + h) : HD * (3 * i + h + 1)].reshape(64, 32, HD) for h in range(3)]) for i in range(3)
    )
    scores = jnp.einsum("htbe,hube->hbtu", q, k, preferred_element_type=jnp.float32) * (1.0 / math.sqrt(HD))
    distance = jnp.abs(frame[:, None] - frame[None, :])
    allowed = distance[None, None, :, :] <= band[:, None, None, None]
    scores = jnp.where(allowed, scores, -jnp.inf)
    highest = jnp.max(scores, axis=-1, keepdims=True)
    e = jnp.exp(scores - highest)
    total = jnp.sum(e, axis=-1, keepdims=True)
    probs = (e / total).astype(jnp.bfloat16)
    result = jnp.einsum("hbtu,hube->htbe", probs, v, preferred_element_type=jnp.float32)
    return result.astype(jnp.bfloat16).reshape(3, 32, 64, HD)


def reorder(blocks, order):
    def kernel(order_ref, in_ref, out_ref):
        def body(i, carry):
            for h in range(3):
                out_ref[i, :, h * HD : h * HD + HD] = in_ref[h, order_ref[i]]
            return carry

        lax.fori_loop(0, 32, body, 0)

    return pl.pallas_call(
        kernel,
        out_shape=jax.ShapeDtypeStruct((32, 64, 384), jnp.bfloat16),
        in_specs=[pl.BlockSpec(memory_space=pltpu.SMEM), pl.BlockSpec(memory_space=pltpu.VMEM)],
        out_specs=pl.BlockSpec(memory_space=pltpu.VMEM),
        compiler_params=pltpu.CompilerParams(vmem_limit_bytes=16 * 2**20),
        name="reorder",
    )(order, blocks)


def spread(blocks, source):
    def kernel(source_ref, in_ref, out_ref):
        def body(z, carry):
            rows = pl.ds(pl.multiple_of(z * 32, 32), 32)
            for g in range(4):
                w = z * 4 + source_ref[g]
                for f in range(2):
                    for i in range(3):
                        column = (4 * i + g) * HD
                        out_ref[f, rows, column : column + HD] = in_ref[w, f * 32 : f * 32 + 32, i * HD : i * HD + HD]
            return carry

        lax.fori_loop(0, 8, body, 0)

    return pl.pallas_call(
        kernel,
        out_shape=jax.ShapeDtypeStruct((2, 256, INNER), jnp.bfloat16),
        in_specs=[pl.BlockSpec(memory_space=pltpu.SMEM), pl.BlockSpec(memory_space=pltpu.VMEM)],
        out_specs=pl.BlockSpec(memory_space=pltpu.VMEM),
        compiler_params=pltpu.CompilerParams(vmem_limit_bytes=16 * 2**20),
        name="spread",
    )(source, blocks)


def per_device(tokens, gain, w_qkv, band):
    z, yl, c, yh, x = (lax.axis_index(n) for n in NAMES)
    kind = yl ^ yh
    normed = normalize(tokens, gain).reshape(2, 8, 32, WIDTH)

    def block(k):
        to = (z + k) % 8
        return lax.dynamic_slice(normed, (0, to, 0, 0), (2, 1, 32, WIDTH)).reshape(64, WIDTH)

    def join(*parts):
        return jnp.concatenate(parts, axis=0)

    unit, more = own_rows(w_qkv, c, yh, x, kind)
    units = gathered(unit)
    lx, rx, far = right(more), left(more), outer(more)
    z1, z7 = shifted(block(1), 1), shifted(block(7), 7)
    step = (lx, rx, far, z1, z7)
    z2, z6 = shifted(after(block(2), *step), 2), shifted(after(block(6), *step), 6)
    i1 = inner(after(join(z1, z7), *step))
    o0, o1 = right(after(lx[:96], *step)), left(after(rx[96:], *step))
    step = (z2, z6, i1, o0, o1)
    z3, z5 = shifted(after(block(3), *step), 3), shifted(after(block(5), *step), 5)
    i2 = inner(after(join(z2, z6, block(0)), *step))
    ready = after(far, *step)
    fl, fr = right(ready), left(ready)
    f0, f1 = right(fl[:96]), left(fr[96:])
    step = (z3, z5, i2, f0, f1)
    z4 = shifted(after(block(4), *step), 4)
    i3 = inner(after(join(z3, z5), *step))
    p1, p2 = join(z1, z7, i1), join(z2, z6, block(0), i2)
    c1, c2 = other_core(after(p1, *step)), other_core(after(p2, *step))

    near, away = yh * 4, (1 - yh) * 4
    l, r, o = (x + 3) % 4, (x + 1) % 4, (x + 2) % 4
    second = jnp.zeros((8, 192, HALF), jnp.bfloat16)
    for v, at, row in (
        (more, near + x, 0),
        (lx, near + l, 0),
        (rx, near + r, 0),
        (o0, near + o, 0),
        (o1, near + o, 96),
        (far, away + x, 0),
        (fl, away + l, 0),
        (fr, away + r, 0),
        (f0, away + o, 0),
        (f1, away + o, 96),
    ):
        second = lax.dynamic_update_slice(second, v[None], (at, row, 0))
    units = after(units, *step)
    got = other_core(pick(units, second, 1 - c, kind))
    mine = pick(units, second, c, kind)
    w = jnp.concatenate([jnp.where(c == 0, mine, got), jnp.where(c == 0, got, mine)], axis=1)

    step = (z4, i3, got, c1, c2)
    i4 = inner(after(z4, *step))
    p3, p4 = join(z3, z5, i3), join(z4, i4)
    c3 = other_core(after(p3, *step))
    c4 = other_core(p4)

    outs, owners, frames = [], [], []
    for group, pair, swap in (((1, 7), p1, c1), ((2, 6, 0), p2, c2), ((3, 5), p3, c3), ((4,), p4, c4)):
        y = lax.dot_general(join(pair, swap), w, (((1,), (1,)), ((), ())), preferred_element_type=jnp.float32)
        outs.append(y.astype(jnp.bfloat16))
        for b in range(2):
            for a in range(2):
                for k in group:
                    owner = ((z - k) % 8) * 4 + (yl ^ a) * 2 + (c ^ b)
                    owners.append(owner)
                    frames += [owner * 2, owner * 2 + 1]
    mine = lax.dynamic_slice(band.reshape(3, 4), (0, kind + 2 * c), (3, 1)).reshape(3)
    result = attend(join(*outs), mine, jnp.stack(frames))
    w = jnp.arange(32, dtype=jnp.int32)
    order = jnp.sum(jnp.where(jnp.stack(owners)[None, :] == w[:, None], w[None, :], 0), axis=1)
    back = lax.all_to_all(reorder(result, order), WIDE, 0, 0, tiled=True)
    g = jnp.arange(4, dtype=jnp.int32)
    return spread(back, ((g % 2) ^ yh) * 2 + g // 2)


def solution(mesh):
    own = Mesh(mesh.devices.reshape(SIZES), NAMES)
    tok = P(WIDE, ("yh", "x"), None)
    placed = (tok, P(), P(None, ("yh", "x")), P())
    return jax.shard_map(per_device, mesh=own, in_specs=placed, out_specs=tok, check_vma=False)
```

```python
import math

import jax
import jax.numpy as jnp
from jax import lax
from jax.experimental import pallas as pl
from jax.experimental.pallas import tpu as pltpu
from jax.sharding import Mesh, PartitionSpec as P

HD = 128
INNER = 1536
WIDTH = 3072
HALF = 1536
EPS = 1e-06
SIZES = (8, 2, 2, 2, 4)
NAMES = ("z", "yl", "c", "yh", "x")
WIDE = ("z", "yl", "c")


def normalize(tokens, gain):
    values = tokens.astype(jnp.float32)
    centered = values - jnp.mean(values, axis=-1, keepdims=True)
    spread = jnp.mean(centered * centered, axis=-1, keepdims=True)
    return (centered * lax.rsqrt(spread + EPS) * gain).astype(jnp.bfloat16)


def send(value, move):
    pairs = []
    for i in range(256):
        z, yl, c, yh, x = i // 32, i // 16 % 2, i // 8 % 2, i // 4 % 2, i % 4
        z, yl, c, yh, x = move(z, yl, c, yh, x)
        pairs.append((i, (((z * 2 + yl) * 2 + c) * 2 + yh) * 4 + x))
    return lax.ppermute(value, NAMES, pairs)


def right(v):
    return send(v, lambda z, yl, c, yh, x: (z, yl, c, yh, (x + 1) % 4))


def left(v):
    return send(v, lambda z, yl, c, yh, x: (z, yl, c, yh, (x + 3) % 4))


def outer(v):
    return send(v, lambda z, yl, c, yh, x: (z, 1 - yl, c, 1 - yh, x))


def inner(v):
    return send(v, lambda z, yl, c, yh, x: (z, 1 - yl, c, yh, x))


def other_core(v):
    return send(v, lambda z, yl, c, yh, x: (z, yl, 1 - c, yh, x))


def shifted(v, k):
    return send(v, lambda z, yl, c, yh, x: ((z + k) % 8, yl, c, yh, x))


def after(value, *done):
    return lax.optimization_barrier((value,) + done)[0]


def own_rows(w, c, yh, x, kind):
    n = yh * 4 + x
    wt = w.T

    def unit(group):
        place = n + (n >= 1 + 2 * group).astype(jnp.int32)
        row = 64 * (2 * (4 * place + group) - 9 * n)
        return lax.dynamic_slice(wt, (row, c * HALF), (128, HALF))

    extra = lax.dynamic_slice(wt, (512 * (1 - n % 2), c * HALF), (64, HALF))
    return jnp.concatenate([unit(kind), unit(kind + 2), extra], axis=0)


def pick(rows, core, kind):
    main = lax.dynamic_slice(rows, (0, 128 * core, 0), (8, 128, HALF))
    rest = lax.dynamic_slice(rows, (2 * (kind + 2 * core), 256, 0), (2, 64, HALF)).reshape(1, 128, HALF)
    spot = 1 + 2 * (kind + 2 * core)
    j = jnp.arange(9, dtype=jnp.int32)[:, None, None]
    early = jnp.concatenate([main, rest], axis=0)
    late = jnp.concatenate([rest, main], axis=0)
    return jnp.where(j < spot, early, jnp.where(j == spot, rest, late)).reshape(1152, HALF)


def attend(qkv, band, frame):
    q, k, v = (
        jnp.stack([qkv[:, HD * (3 * i + h) : HD * (3 * i + h + 1)].reshape(64, 32, HD) for h in range(3)]) for i in range(3)
    )
    scores = jnp.einsum("htbe,hube->hbtu", q, k, preferred_element_type=jnp.float32) * (1.0 / math.sqrt(HD))
    distance = jnp.abs(frame[:, None] - frame[None, :])
    allowed = distance[None, None, :, :] <= band[:, None, None, None]
    scores = jnp.where(allowed, scores, -jnp.inf)
    highest = jnp.max(scores, axis=-1, keepdims=True)
    e = jnp.exp(scores - highest)
    total = jnp.sum(e, axis=-1, keepdims=True)
    probs = (e / total).astype(jnp.bfloat16)
    result = jnp.einsum("hbtu,hube->htbe", probs, v, preferred_element_type=jnp.float32)
    return result.astype(jnp.bfloat16).reshape(3, 32, 64, HD)


def reorder(blocks, order):
    def kernel(order_ref, in_ref, out_ref):
        def body(i, carry):
            for h in range(3):
                out_ref[i, :, h * HD : h * HD + HD] = in_ref[h, order_ref[i]]
            return carry

        lax.fori_loop(0, 32, body, 0)

    return pl.pallas_call(
        kernel,
        out_shape=jax.ShapeDtypeStruct((32, 64, 384), jnp.bfloat16),
        in_specs=[pl.BlockSpec(memory_space=pltpu.SMEM), pl.BlockSpec(memory_space=pltpu.VMEM)],
        out_specs=pl.BlockSpec(memory_space=pltpu.VMEM),
        compiler_params=pltpu.CompilerParams(vmem_limit_bytes=16 * 2**20),
        name="reorder",
    )(order, blocks)


def spread(blocks, source):
    def kernel(source_ref, in_ref, out_ref):
        def body(z, carry):
            rows = pl.ds(pl.multiple_of(z * 32, 32), 32)
            for g in range(4):
                w = z * 4 + source_ref[g]
                for f in range(2):
                    for i in range(3):
                        column = (4 * i + g) * HD
                        out_ref[f, rows, column : column + HD] = in_ref[w, f * 32 : f * 32 + 32, i * HD : i * HD + HD]
            return carry

        lax.fori_loop(0, 8, body, 0)

    return pl.pallas_call(
        kernel,
        out_shape=jax.ShapeDtypeStruct((2, 256, INNER), jnp.bfloat16),
        in_specs=[pl.BlockSpec(memory_space=pltpu.SMEM), pl.BlockSpec(memory_space=pltpu.VMEM)],
        out_specs=pl.BlockSpec(memory_space=pltpu.VMEM),
        compiler_params=pltpu.CompilerParams(vmem_limit_bytes=16 * 2**20),
        name="spread",
    )(source, blocks)


def per_device(tokens, gain, w_qkv, band):
    z, yl, c, yh, x = (lax.axis_index(n) for n in NAMES)
    kind = yl ^ yh
    normed = normalize(tokens, gain).reshape(2, 8, 32, WIDTH)

    def block(k):
        to = (z + k) % 8
        return lax.dynamic_slice(normed, (0, to, 0, 0), (2, 1, 32, WIDTH)).reshape(64, WIDTH)

    def join(*parts):
        return jnp.concatenate(parts, axis=0)

    def project(part, w):
        y = lax.dot_general(part, w, (((1,), (1,)), ((), ())), preferred_element_type=jnp.float32)
        return y.astype(jnp.bfloat16)

    hold = lax.optimization_barrier
    own = own_rows(w_qkv, c, yh, x, kind)
    far = outer(own)
    lx, rx = right(own), left(own)
    z1, z7 = shifted(block(1), 1), shifted(block(7), 7)
    z1, z7, j1, toright, toleft, b3, b5 = hold(
        (z1, z7, join(z1, z7, block(0)), join(lx[:160], far[:160]), join(rx[160:], far[160:]), block(3), block(5))
    )
    i1 = inner(j1)
    l2, r2 = right(toright), left(toleft)
    z3, z5 = shifted(b3, 3), shifted(b5, 5)
    z3, z5, j3, toright, toleft, b2, b6, i1 = hold(
        (z3, z5, join(z3, z5), join(l2[160:], far[160:]), join(r2[160:], far[:160]), block(2), block(6), i1)
    )
    i3 = inner(j3)
    l3, r3 = right(toright), left(toleft)
    z2, z6 = shifted(b2, 2), shifted(b6, 6)

    near, away = yh * 4, (1 - yh) * 4
    l, r, o = (x + 3) % 4, (x + 1) % 4, (x + 2) % 4
    rows = jnp.zeros((8, 320, HALF), jnp.bfloat16)
    for v, at, row in (
        (own, near + x, 0),
        (lx, near + l, 0),
        (rx, near + r, 0),
        (far, away + x, 0),
        (l2[:160], near + o, 0),
        (r2[:160], near + o, 160),
        (l2[160:], away + l, 0),
        (r2[160:], away + r, 160),
        (l3[:160], away + o, 0),
        (r3[:160], away + o, 160),
        (l3[160:], away + l, 160),
        (r3[160:], away + r, 0),
    ):
        rows = lax.dynamic_update_slice(rows, v[None], (at, row, 0))
    theirs, mine = pick(rows, 1 - c, kind), pick(rows, c, kind)
    j2, theirs, mine, p1, b4, i3 = hold((join(z2, z6), theirs, mine, join(j1, i1), block(4), i3))
    c1, got = other_core(p1), other_core(theirs)
    i2 = inner(j2)
    z4 = shifted(b4, 4)
    p3 = join(j3, i3)
    c3 = other_core(p3)
    w = jnp.concatenate([jnp.where(c == 0, mine, got), jnp.where(c == 0, got, mine)], axis=1)
    y1, x1 = project(p1, w), project(c1, w)
    z4, y1, x1, i2 = hold((z4, y1, x1, i2))
    i4 = inner(z4)
    p2 = join(j2, i2)
    c2 = other_core(p2)
    y3, x3 = project(p3, w), project(c3, w)
    i4, y3, x3 = hold((i4, y3, x3))
    p4 = join(z4, i4)
    c4 = other_core(p4)
    y2, x2 = project(p2, w), project(c2, w)
    y4, x4 = project(p4, w), project(c4, w)

    outs, owners, frames = [y1, x1, y3, x3, y2, x2, y4, x4], [], []
    for group in ((1, 7, 0), (3, 5), (2, 6), (4,)):
        for b in range(2):
            for a in range(2):
                for k in group:
                    owner = ((z - k) % 8) * 4 + (yl ^ a) * 2 + (c ^ b)
                    owners.append(owner)
                    frames += [owner * 2, owner * 2 + 1]
    mine = lax.dynamic_slice(band.reshape(3, 4), (0, kind + 2 * c), (3, 1)).reshape(3)
    result = attend(join(*outs), mine, jnp.stack(frames))
    w = jnp.arange(32, dtype=jnp.int32)
    order = jnp.sum(jnp.where(jnp.stack(owners)[None, :] == w[:, None], w[None, :], 0), axis=1)
    back = lax.all_to_all(reorder(result, order), WIDE, 0, 0, tiled=True)
    g = jnp.arange(4, dtype=jnp.int32)
    return spread(back, ((g % 2) ^ yh) * 2 + g // 2)


def solution(mesh):
    own = Mesh(mesh.devices.reshape(SIZES), NAMES)
    tok = P(WIDE, ("yh", "x"), None)
    placed = (tok, P(), P(None, ("yh", "x")), P())
    return jax.shard_map(per_device, mesh=own, in_specs=placed, out_specs=tok, check_vma=False)
```

```python
import math

import jax
import jax.numpy as jnp
from jax import lax
from jax.experimental import pallas as pl
from jax.experimental.pallas import tpu as pltpu
from jax.sharding import Mesh, PartitionSpec as P

HD = 128
INNER = 1536
WIDTH = 3072
HALF = 1536
EPS = 1e-06
SIZES = (8, 2, 2, 2, 4)
NAMES = ("z", "yl", "c", "yh", "x")
WIDE = ("z", "yl", "c")


def normalize(tokens, gain):
    values = tokens.astype(jnp.float32)
    centered = values - jnp.mean(values, axis=-1, keepdims=True)
    spread = jnp.mean(centered * centered, axis=-1, keepdims=True)
    return (centered * lax.rsqrt(spread + EPS) * gain).astype(jnp.bfloat16)


def send(value, move):
    pairs = []
    for i in range(256):
        z, yl, c, yh, x = i // 32, i // 16 % 2, i // 8 % 2, i // 4 % 2, i % 4
        z, yl, c, yh, x = move(z, yl, c, yh, x)
        pairs.append((i, (((z * 2 + yl) * 2 + c) * 2 + yh) * 4 + x))
    return lax.ppermute(value, NAMES, pairs)


def right(v):
    return send(v, lambda z, yl, c, yh, x: (z, yl, c, yh, (x + 1) % 4))


def left(v):
    return send(v, lambda z, yl, c, yh, x: (z, yl, c, yh, (x + 3) % 4))


def outer(v):
    return send(v, lambda z, yl, c, yh, x: (z, 1 - yl, c, 1 - yh, x))


def inner(v):
    return send(v, lambda z, yl, c, yh, x: (z, 1 - yl, c, yh, x))


def other_core(v):
    return send(v, lambda z, yl, c, yh, x: (z, yl, 1 - c, yh, x))


def shifted(v, k):
    return send(v, lambda z, yl, c, yh, x: ((z + k) % 8, yl, c, yh, x))


def after(value, *done):
    return lax.optimization_barrier((value,) + done)[0]


def own_rows(w, c, yh, x, kind):
    n = yh * 4 + x
    wt = w.T

    def unit(group):
        place = n + (n >= 1 + 2 * group).astype(jnp.int32)
        row = 64 * (2 * (4 * place + group) - 9 * n)
        return lax.dynamic_slice(wt, (row, c * HALF), (128, HALF))

    extra = lax.dynamic_slice(wt, (512 * (1 - n % 2), c * HALF), (64, HALF))
    return jnp.concatenate([unit(kind), unit(kind + 2), extra], axis=0)


def pick(rows, core, kind):
    main = lax.dynamic_slice(rows, (0, 128 * core, 0), (8, 128, HALF))
    rest = lax.dynamic_slice(rows, (2 * (kind + 2 * core), 256, 0), (2, 64, HALF)).reshape(1, 128, HALF)
    spot = 1 + 2 * (kind + 2 * core)
    j = jnp.arange(9, dtype=jnp.int32)[:, None, None]
    early = jnp.concatenate([main, rest], axis=0)
    late = jnp.concatenate([rest, main], axis=0)
    return jnp.where(j < spot, early, jnp.where(j == spot, rest, late)).reshape(1152, HALF)


def attend(qkv, band, frame):
    q, k, v = (
        jnp.stack([qkv[:, HD * (3 * i + h) : HD * (3 * i + h + 1)].reshape(64, 32, HD) for h in range(3)]) for i in range(3)
    )
    scores = jnp.einsum("htbe,hube->hbtu", q, k, preferred_element_type=jnp.float32) * (1.0 / math.sqrt(HD))
    distance = jnp.abs(frame[:, None] - frame[None, :])
    allowed = distance[None, None, :, :] <= band[:, None, None, None]
    scores = jnp.where(allowed, scores, -jnp.inf)
    highest = jnp.max(scores, axis=-1, keepdims=True)
    e = jnp.exp(scores - highest)
    total = jnp.sum(e, axis=-1, keepdims=True)
    probs = (e / total).astype(jnp.bfloat16)
    result = jnp.einsum("hbtu,hube->htbe", probs, v, preferred_element_type=jnp.float32)
    return result.astype(jnp.bfloat16).reshape(3, 32, 64, HD)


def reorder(blocks, order):
    def kernel(order_ref, in_ref, out_ref):
        def body(i, carry):
            for h in range(3):
                out_ref[i, :, h * HD : h * HD + HD] = in_ref[h, order_ref[i]]
            return carry

        lax.fori_loop(0, 32, body, 0)

    return pl.pallas_call(
        kernel,
        out_shape=jax.ShapeDtypeStruct((32, 64, 384), jnp.bfloat16),
        in_specs=[pl.BlockSpec(memory_space=pltpu.SMEM), pl.BlockSpec(memory_space=pltpu.VMEM)],
        out_specs=pl.BlockSpec(memory_space=pltpu.VMEM),
        compiler_params=pltpu.CompilerParams(vmem_limit_bytes=16 * 2**20),
        name="reorder",
    )(order, blocks)


def spread(blocks, source):
    def kernel(source_ref, in_ref, out_ref):
        def body(z, carry):
            rows = pl.ds(pl.multiple_of(z * 32, 32), 32)
            for g in range(4):
                w = z * 4 + source_ref[g]
                for f in range(2):
                    for i in range(3):
                        column = (4 * i + g) * HD
                        out_ref[f, rows, column : column + HD] = in_ref[w, f * 32 : f * 32 + 32, i * HD : i * HD + HD]
            return carry

        lax.fori_loop(0, 8, body, 0)

    return pl.pallas_call(
        kernel,
        out_shape=jax.ShapeDtypeStruct((2, 256, INNER), jnp.bfloat16),
        in_specs=[pl.BlockSpec(memory_space=pltpu.SMEM), pl.BlockSpec(memory_space=pltpu.VMEM)],
        out_specs=pl.BlockSpec(memory_space=pltpu.VMEM),
        compiler_params=pltpu.CompilerParams(vmem_limit_bytes=16 * 2**20),
        name="spread",
    )(source, blocks)


def per_device(tokens, gain, w_qkv, band):
    z, yl, c, yh, x = (lax.axis_index(n) for n in NAMES)
    kind = yl ^ yh
    normed = normalize(tokens, gain).reshape(2, 8, 32, WIDTH)

    def block(k):
        to = (z + k) % 8
        return lax.dynamic_slice(normed, (0, to, 0, 0), (2, 1, 32, WIDTH)).reshape(64, WIDTH)

    def join(*parts):
        return jnp.concatenate(parts, axis=0)

    def project(part, w):
        y = lax.dot_general(part, w, (((1,), (1,)), ((), ())), preferred_element_type=jnp.float32)
        return y.astype(jnp.bfloat16)

    hold = lax.optimization_barrier
    own = own_rows(w_qkv, c, yh, x, kind)
    far = outer(own)
    lx, rx = right(own), left(own)
    z1, z7 = shifted(block(1), 1), shifted(block(7), 7)
    z1, z7, j1, toright, toleft, b3, b5 = hold(
        (z1, z7, join(z1, z7, block(0)), join(lx[:160], far), join(rx[160:], far), block(3), block(5))
    )
    i1 = inner(j1)
    l2, r2 = right(toright), left(toleft)
    z3, z5 = shifted(b3, 3), shifted(b5, 5)
    z3, z5, j3, toright, toleft, b2, b6, i1 = hold(
        (z3, z5, join(z3, z5), l2[160:320], r2[320:], block(2), block(6), i1)
    )
    i3 = inner(j3)
    l3, r3 = right(toright), left(toleft)
    z2, z6 = shifted(b2, 2), shifted(b6, 6)

    near, away = yh * 4, (1 - yh) * 4
    l, r, o = (x + 3) % 4, (x + 1) % 4, (x + 2) % 4
    rows = jnp.zeros((8, 320, HALF), jnp.bfloat16)
    for v, at, row in (
        (own, near + x, 0),
        (lx, near + l, 0),
        (rx, near + r, 0),
        (far, away + x, 0),
        (l2[:160], near + o, 0),
        (r2[:160], near + o, 160),
        (l2[160:], away + l, 0),
        (r2[160:], away + r, 0),
        (l3, away + o, 0),
        (r3, away + o, 160),
    ):
        rows = lax.dynamic_update_slice(rows, v[None], (at, row, 0))
    theirs, mine = pick(rows, 1 - c, kind), pick(rows, c, kind)
    j2, theirs, mine, p1, b4, i3 = hold((join(z2, z6), theirs, mine, join(j1, i1), block(4), i3))
    c1, got = other_core(p1), other_core(theirs)
    i2 = inner(j2)
    z4 = shifted(b4, 4)
    w = jnp.concatenate([jnp.where(c == 0, mine, got), jnp.where(c == 0, got, mine)], axis=1)
    y1, x1 = project(p1, w), project(c1, w)
    z4, y1, x1, i2, p3 = hold((z4, y1, x1, i2, join(j3, i3)))
    i4 = inner(z4)
    p2 = join(j2, i2)
    c3, c2 = other_core(p3), other_core(p2)
    y3, x3 = project(p3, w), project(c3, w)
    y2, x2 = project(p2, w), project(c2, w)
    i4, y3, x3, y2, x2 = hold((i4, y3, x3, y2, x2))
    p4 = join(z4, i4)
    c4 = other_core(p4)
    y4, x4 = project(p4, w), project(c4, w)

    outs, owners, frames = [y1, x1, y3, x3, y2, x2, y4, x4], [], []
    for group in ((1, 7, 0), (3, 5), (2, 6), (4,)):
        for b in range(2):
            for a in range(2):
                for k in group:
                    owner = ((z - k) % 8) * 4 + (yl ^ a) * 2 + (c ^ b)
                    owners.append(owner)
                    frames += [owner * 2, owner * 2 + 1]
    mine = lax.dynamic_slice(band.reshape(3, 4), (0, kind + 2 * c), (3, 1)).reshape(3)
    result = attend(join(*outs), mine, jnp.stack(frames))
    w = jnp.arange(32, dtype=jnp.int32)
    order = jnp.sum(jnp.where(jnp.stack(owners)[None, :] == w[:, None], w[None, :], 0), axis=1)
    back = lax.all_to_all(reorder(result, order), WIDE, 0, 0, tiled=True)
    g = jnp.arange(4, dtype=jnp.int32)
    return spread(back, ((g % 2) ^ yh) * 2 + g // 2)


def solution(mesh):
    own = Mesh(mesh.devices.reshape(SIZES), NAMES)
    tok = P(WIDE, ("yh", "x"), None)
    placed = (tok, P(), P(None, ("yh", "x")), P())
    return jax.shard_map(per_device, mesh=own, in_specs=placed, out_specs=tok, check_vma=False)
```

```python
import math

import jax
import jax.numpy as jnp
from jax import lax
from jax.experimental import pallas as pl
from jax.experimental.pallas import tpu as pltpu
from jax.sharding import Mesh, PartitionSpec as P

HD = 128
INNER = 1536
WIDTH = 3072
HALF = 1536
EPS = 1e-06
SIZES = (8, 2, 2, 2, 4)
NAMES = ("z", "yl", "c", "yh", "x")
WIDE = ("z", "yl", "c")


def normalize(tokens, gain):
    values = tokens.astype(jnp.float32)
    centered = values - jnp.mean(values, axis=-1, keepdims=True)
    spread = jnp.mean(centered * centered, axis=-1, keepdims=True)
    return (centered * lax.rsqrt(spread + EPS) * gain).astype(jnp.bfloat16)


def send(value, move):
    pairs = []
    for i in range(256):
        z, yl, c, yh, x = i // 32, i // 16 % 2, i // 8 % 2, i // 4 % 2, i % 4
        z, yl, c, yh, x = move(z, yl, c, yh, x)
        pairs.append((i, (((z * 2 + yl) * 2 + c) * 2 + yh) * 4 + x))
    return lax.ppermute(value, NAMES, pairs)


def right(v):
    return send(v, lambda z, yl, c, yh, x: (z, yl, c, yh, (x + 1) % 4))


def left(v):
    return send(v, lambda z, yl, c, yh, x: (z, yl, c, yh, (x + 3) % 4))


def outer(v):
    return send(v, lambda z, yl, c, yh, x: (z, 1 - yl, c, 1 - yh, x))


def inner(v):
    return send(v, lambda z, yl, c, yh, x: (z, 1 - yl, c, yh, x))


def other_core(v):
    return send(v, lambda z, yl, c, yh, x: (z, yl, 1 - c, yh, x))


def shifted(v, k):
    return send(v, lambda z, yl, c, yh, x: ((z + k) % 8, yl, c, yh, x))


def after(value, *done):
    return lax.optimization_barrier((value,) + done)[0]


def own_rows(w, c, yh, x, kind):
    n = yh * 4 + x
    wt = w.T

    def unit(group):
        place = n + (n >= 1 + 2 * group).astype(jnp.int32)
        row = 64 * (2 * (4 * place + group) - 9 * n)
        return lax.dynamic_slice(wt, (row, c * HALF), (128, HALF))

    extra = lax.dynamic_slice(wt, (512 * (1 - n % 2), c * HALF), (64, HALF))
    return jnp.concatenate([unit(kind), unit(kind + 2), extra], axis=0)


def pick(rows, core, kind):
    main = lax.dynamic_slice(rows, (0, 128 * core, 0), (8, 128, HALF))
    rest = lax.dynamic_slice(rows, (2 * (kind + 2 * core), 256, 0), (2, 64, HALF)).reshape(1, 128, HALF)
    spot = 1 + 2 * (kind + 2 * core)
    j = jnp.arange(9, dtype=jnp.int32)[:, None, None]
    early = jnp.concatenate([main, rest], axis=0)
    late = jnp.concatenate([rest, main], axis=0)
    return jnp.where(j < spot, early, jnp.where(j == spot, rest, late)).reshape(1152, HALF)


def attend(qkv, band, frame):
    q, k, v = (
        jnp.stack([qkv[:, HD * (3 * i + h) : HD * (3 * i + h + 1)].reshape(64, 32, HD) for h in range(3)]) for i in range(3)
    )
    scores = jnp.einsum("htbe,hube->hbtu", q, k, preferred_element_type=jnp.float32) * (1.0 / math.sqrt(HD))
    distance = jnp.abs(frame[:, None] - frame[None, :])
    allowed = distance[None, None, :, :] <= band[:, None, None, None]
    scores = jnp.where(allowed, scores, -jnp.inf)
    highest = jnp.max(scores, axis=-1, keepdims=True)
    e = jnp.exp(scores - highest)
    total = jnp.sum(e, axis=-1, keepdims=True)
    probs = (e / total).astype(jnp.bfloat16)
    result = jnp.einsum("hbtu,hube->htbe", probs, v, preferred_element_type=jnp.float32)
    return result.astype(jnp.bfloat16).reshape(3, 32, 64, HD)


def reorder(blocks, order):
    def kernel(order_ref, in_ref, out_ref):
        def body(i, carry):
            for h in range(3):
                out_ref[i, :, h * HD : h * HD + HD] = in_ref[h, order_ref[i]]
            return carry

        lax.fori_loop(0, 32, body, 0)

    return pl.pallas_call(
        kernel,
        out_shape=jax.ShapeDtypeStruct((32, 64, 384), jnp.bfloat16),
        in_specs=[pl.BlockSpec(memory_space=pltpu.SMEM), pl.BlockSpec(memory_space=pltpu.VMEM)],
        out_specs=pl.BlockSpec(memory_space=pltpu.VMEM),
        compiler_params=pltpu.CompilerParams(vmem_limit_bytes=16 * 2**20),
        name="reorder",
    )(order, blocks)


def spread(blocks, source):
    def kernel(source_ref, in_ref, out_ref):
        def body(z, carry):
            rows = pl.ds(pl.multiple_of(z * 32, 32), 32)
            for g in range(4):
                w = z * 4 + source_ref[g]
                for f in range(2):
                    for i in range(3):
                        column = (4 * i + g) * HD
                        out_ref[f, rows, column : column + HD] = in_ref[w, f * 32 : f * 32 + 32, i * HD : i * HD + HD]
            return carry

        lax.fori_loop(0, 8, body, 0)

    return pl.pallas_call(
        kernel,
        out_shape=jax.ShapeDtypeStruct((2, 256, INNER), jnp.bfloat16),
        in_specs=[pl.BlockSpec(memory_space=pltpu.SMEM), pl.BlockSpec(memory_space=pltpu.VMEM)],
        out_specs=pl.BlockSpec(memory_space=pltpu.VMEM),
        compiler_params=pltpu.CompilerParams(vmem_limit_bytes=16 * 2**20),
        name="spread",
    )(source, blocks)


def per_device(tokens, gain, w_qkv, band):
    z, yl, c, yh, x = (lax.axis_index(n) for n in NAMES)
    kind = yl ^ yh
    normed = normalize(tokens, gain).reshape(2, 8, 32, WIDTH)

    def block(k):
        to = (z + k) % 8
        return lax.dynamic_slice(normed, (0, to, 0, 0), (2, 1, 32, WIDTH)).reshape(64, WIDTH)

    def join(*parts):
        return jnp.concatenate(parts, axis=0)

    def project(part, w):
        y = lax.dot_general(part, w, (((1,), (1,)), ((), ())), preferred_element_type=jnp.float32)
        return y.astype(jnp.bfloat16)

    hold = lax.optimization_barrier
    own = own_rows(w_qkv, c, yh, x, kind)
    far = outer(own)
    lx, rx = right(own), left(own)
    z1, z7 = shifted(block(1), 1), shifted(block(7), 7)
    z1, z7, j1, toright, toleft, b3, b5 = hold(
        (z1, z7, join(z1, z7, block(0)), join(lx[:160], far), join(rx[160:], far), block(3), block(5))
    )
    i1 = inner(j1)
    l2, r2 = right(toright), left(toleft)
    z3, z5 = shifted(b3, 3), shifted(b5, 5)
    z3, z5, j3, toright, toleft, b2, b6, i1 = hold(
        (z3, z5, join(z3, z5), l2[160:320], r2[320:], block(2), block(6), i1)
    )
    i3 = inner(j3)
    l3, r3 = right(toright), left(toleft)
    z2, z6 = shifted(b2, 2), shifted(b6, 6)

    near, away = yh * 4, (1 - yh) * 4
    l, r, o = (x + 3) % 4, (x + 1) % 4, (x + 2) % 4
    rows = jnp.zeros((8, 320, HALF), jnp.bfloat16)
    for v, at, row in (
        (own, near + x, 0),
        (lx, near + l, 0),
        (rx, near + r, 0),
        (far, away + x, 0),
        (l2[:160], near + o, 0),
        (r2[:160], near + o, 160),
        (l2[160:], away + l, 0),
        (r2[160:], away + r, 0),
        (l3, away + o, 0),
        (r3, away + o, 160),
    ):
        rows = lax.dynamic_update_slice(rows, v[None], (at, row, 0))
    theirs, mine = pick(rows, 1 - c, kind), pick(rows, c, kind)
    j2, theirs, p1, b4, p3 = hold((join(z2, z6), theirs, join(j1, i1), block(4), join(j3, i3)))
    c1, got = other_core(p1), other_core(theirs)
    i2 = inner(j2)
    z4 = shifted(b4, 4)
    w = jnp.concatenate([jnp.where(c == 0, mine, got), jnp.where(c == 0, got, mine)], axis=1)
    y1, x1 = project(p1, w), project(c1, w)
    z4, y1, x1, i2 = hold((z4, y1, x1, i2))
    i4 = inner(z4)
    p2 = join(j2, i2)
    c3, c2 = other_core(p3), other_core(p2)
    y3, x3 = project(p3, w), project(c3, w)
    y2, x2 = project(p2, w), project(c2, w)
    i4, y3, x3, y2, x2 = hold((i4, y3, x3, y2, x2))
    p4 = join(z4, i4)
    c4 = other_core(p4)
    y4, x4 = project(p4, w), project(c4, w)

    outs, owners, frames = [y1, x1, y3, x3, y2, x2, y4, x4], [], []
    for group in ((1, 7, 0), (3, 5), (2, 6), (4,)):
        for b in range(2):
            for a in range(2):
                for k in group:
                    owner = ((z - k) % 8) * 4 + (yl ^ a) * 2 + (c ^ b)
                    owners.append(owner)
                    frames += [owner * 2, owner * 2 + 1]
    mine = lax.dynamic_slice(band.reshape(3, 4), (0, kind + 2 * c), (3, 1)).reshape(3)
    result = attend(join(*outs), mine, jnp.stack(frames))
    w = jnp.arange(32, dtype=jnp.int32)
    order = jnp.sum(jnp.where(jnp.stack(owners)[None, :] == w[:, None], w[None, :], 0), axis=1)
    back = lax.all_to_all(reorder(result, order), WIDE, 0, 0, tiled=True)
    g = jnp.arange(4, dtype=jnp.int32)
    return spread(back, ((g % 2) ^ yh) * 2 + g // 2)


def solution(mesh):
    own = Mesh(mesh.devices.reshape(SIZES), NAMES)
    tok = P(WIDE, ("yh", "x"), None)
    placed = (tok, P(), P(None, ("yh", "x")), P())
    return jax.shard_map(per_device, mesh=own, in_specs=placed, out_specs=tok, check_vma=False)
```

```python
import math

import jax
import jax.numpy as jnp
from jax import lax
from jax.experimental import pallas as pl
from jax.experimental.pallas import tpu as pltpu
from jax.sharding import Mesh, PartitionSpec as P

HD = 128
INNER = 1536
WIDTH = 3072
HALF = 1536
EPS = 1e-06
SIZES = (8, 2, 2, 2, 4)
NAMES = ("z", "yl", "c", "yh", "x")
WIDE = ("z", "yl", "c")


def normalize(tokens, gain):
    values = tokens.astype(jnp.float32)
    centered = values - jnp.mean(values, axis=-1, keepdims=True)
    spread = jnp.mean(centered * centered, axis=-1, keepdims=True)
    return (centered * lax.rsqrt(spread + EPS) * gain).astype(jnp.bfloat16)


def send(value, move):
    pairs = []
    for i in range(256):
        z, yl, c, yh, x = i // 32, i // 16 % 2, i // 8 % 2, i // 4 % 2, i % 4
        z, yl, c, yh, x = move(z, yl, c, yh, x)
        pairs.append((i, (((z * 2 + yl) * 2 + c) * 2 + yh) * 4 + x))
    return lax.ppermute(value, NAMES, pairs)


def right(v):
    return send(v, lambda z, yl, c, yh, x: (z, yl, c, yh, (x + 1) % 4))


def left(v):
    return send(v, lambda z, yl, c, yh, x: (z, yl, c, yh, (x + 3) % 4))


def outer(v):
    return send(v, lambda z, yl, c, yh, x: (z, 1 - yl, c, 1 - yh, x))


def inner(v):
    return send(v, lambda z, yl, c, yh, x: (z, 1 - yl, c, yh, x))


def other_core(v):
    return send(v, lambda z, yl, c, yh, x: (z, yl, 1 - c, yh, x))


def shifted(v, k):
    return send(v, lambda z, yl, c, yh, x: ((z + k) % 8, yl, c, yh, x))


def after(value, *done):
    return lax.optimization_barrier((value,) + done)[0]


def own_rows(w, c, yh, x, kind):
    n = yh * 4 + x
    wt = w.T

    def unit(group):
        place = n + (n >= 1 + 2 * group).astype(jnp.int32)
        row = 64 * (2 * (4 * place + group) - 9 * n)
        return lax.dynamic_slice(wt, (row, c * HALF), (128, HALF))

    extra = lax.dynamic_slice(wt, (512 * (1 - n % 2), c * HALF), (64, HALF))
    return jnp.concatenate([unit(kind), unit(kind + 2), extra], axis=0)


def pick(rows, core, kind):
    main = lax.dynamic_slice(rows, (0, 128 * core, 0), (8, 128, HALF))
    rest = lax.dynamic_slice(rows, (2 * (kind + 2 * core), 256, 0), (2, 64, HALF)).reshape(1, 128, HALF)
    spot = 1 + 2 * (kind + 2 * core)
    j = jnp.arange(9, dtype=jnp.int32)[:, None, None]
    early = jnp.concatenate([main, rest], axis=0)
    late = jnp.concatenate([rest, main], axis=0)
    return jnp.where(j < spot, early, jnp.where(j == spot, rest, late)).reshape(1152, HALF)


def attend(qkv, band, frame):
    q, k, v = (
        jnp.stack([qkv[:, HD * (3 * i + h) : HD * (3 * i + h + 1)].reshape(64, 32, HD) for h in range(3)]) for i in range(3)
    )
    scores = jnp.einsum("htbe,hube->hbtu", q, k, preferred_element_type=jnp.float32) * (1.0 / math.sqrt(HD))
    distance = jnp.abs(frame[:, None] - frame[None, :])
    allowed = distance[None, None, :, :] <= band[:, None, None, None]
    scores = jnp.where(allowed, scores, -jnp.inf)
    highest = jnp.max(scores, axis=-1, keepdims=True)
    e = jnp.exp(scores - highest)
    total = jnp.sum(e, axis=-1, keepdims=True)
    probs = (e / total).astype(jnp.bfloat16)
    result = jnp.einsum("hbtu,hube->htbe", probs, v, preferred_element_type=jnp.float32)
    return result.astype(jnp.bfloat16).reshape(3, 32, 64, HD)


def reorder(blocks, order):
    def kernel(order_ref, in_ref, out_ref):
        def body(i, carry):
            for h in range(3):
                out_ref[i, :, h * HD : h * HD + HD] = in_ref[h, order_ref[i]]
            return carry

        lax.fori_loop(0, 32, body, 0)

    return pl.pallas_call(
        kernel,
        out_shape=jax.ShapeDtypeStruct((32, 64, 384), jnp.bfloat16),
        in_specs=[pl.BlockSpec(memory_space=pltpu.SMEM), pl.BlockSpec(memory_space=pltpu.VMEM)],
        out_specs=pl.BlockSpec(memory_space=pltpu.VMEM),
        compiler_params=pltpu.CompilerParams(vmem_limit_bytes=16 * 2**20),
        name="reorder",
    )(order, blocks)


def spread(blocks, source):
    def kernel(source_ref, in_ref, out_ref):
        def body(z, carry):
            rows = pl.ds(pl.multiple_of(z * 32, 32), 32)
            for g in range(4):
                w = z * 4 + source_ref[g]
                for f in range(2):
                    for i in range(3):
                        column = (4 * i + g) * HD
                        out_ref[f, rows, column : column + HD] = in_ref[w, f * 32 : f * 32 + 32, i * HD : i * HD + HD]
            return carry

        lax.fori_loop(0, 8, body, 0)

    return pl.pallas_call(
        kernel,
        out_shape=jax.ShapeDtypeStruct((2, 256, INNER), jnp.bfloat16),
        in_specs=[pl.BlockSpec(memory_space=pltpu.SMEM), pl.BlockSpec(memory_space=pltpu.VMEM)],
        out_specs=pl.BlockSpec(memory_space=pltpu.VMEM),
        compiler_params=pltpu.CompilerParams(vmem_limit_bytes=16 * 2**20),
        name="spread",
    )(source, blocks)


def per_device(tokens, gain, w_qkv, band):
    z, yl, c, yh, x = (lax.axis_index(n) for n in NAMES)
    kind = yl ^ yh
    normed = normalize(tokens, gain).reshape(2, 8, 32, WIDTH)

    def block(k):
        to = (z + k) % 8
        return lax.dynamic_slice(normed, (0, to, 0, 0), (2, 1, 32, WIDTH)).reshape(64, WIDTH)

    def join(*parts):
        return jnp.concatenate(parts, axis=0)

    def project(part, w):
        y = lax.dot_general(part, w, (((1,), (1,)), ((), ())), preferred_element_type=jnp.float32)
        return y.astype(jnp.bfloat16)

    hold = lax.optimization_barrier
    own = own_rows(w_qkv, c, yh, x, kind)
    far = outer(own)
    lx, rx = right(own), left(own)
    z1, z7 = shifted(block(1), 1), shifted(block(7), 7)
    z1, z7, j1, toright, toleft, b3, b5 = hold(
        (z1, z7, join(z1, z7, block(0)), join(lx[:160], far), join(rx[160:], far), block(3), block(5))
    )
    i1 = inner(j1)
    l2, r2 = right(toright), left(toleft)
    z3, z5 = shifted(b3, 3), shifted(b5, 5)
    z3, z5, j3, toright, toleft, b2, b6, i1 = hold(
        (z3, z5, join(z3, z5), l2[160:320], r2[320:], block(2), block(6), i1)
    )
    i3 = inner(j3)
    l3, r3 = right(toright), left(toleft)
    z2, z6 = shifted(b2, 2), shifted(b6, 6)

    near, away = yh * 4, (1 - yh) * 4
    l, r, o = (x + 3) % 4, (x + 1) % 4, (x + 2) % 4
    rows = jnp.zeros((8, 320, HALF), jnp.bfloat16)
    for v, at, row in (
        (own, near + x, 0),
        (lx, near + l, 0),
        (rx, near + r, 0),
        (far, away + x, 0),
        (l2[:160], near + o, 0),
        (r2[:160], near + o, 160),
        (l2[160:], away + l, 0),
        (r2[160:], away + r, 0),
        (l3, away + o, 0),
        (r3, away + o, 160),
    ):
        rows = lax.dynamic_update_slice(rows, v[None], (at, row, 0))
    theirs, mine = pick(rows, 1 - c, kind), pick(rows, c, kind)
    j2, theirs, p1, b4, i3 = hold((join(z2, z6), theirs, join(j1, i1), block(4), i3))
    c1, got = other_core(p1), other_core(theirs)
    i2 = inner(j2)
    z4 = shifted(b4, 4)
    w = jnp.concatenate([jnp.where(c == 0, mine, got), jnp.where(c == 0, got, mine)], axis=1)
    y1, x1 = project(p1, w), project(c1, w)
    z4, y1, x1, i2, p3 = hold((z4, y1, x1, i2, join(j3, i3)))
    i4 = inner(z4)
    p2 = join(j2, i2)
    c3, c2 = other_core(p3), other_core(p2)
    y3, x3 = project(p3, w), project(c3, w)
    y2, x2 = project(p2, w), project(c2, w)
    i4, y3, x3, y2, x2 = hold((i4, y3, x3, y2, x2))
    p4 = join(z4, i4)
    c4 = other_core(p4)
    y4, x4 = project(p4, w), project(c4, w)

    outs, owners, frames = [y1, x1, y3, x3, y2, x2, y4, x4], [], []
    for group in ((1, 7, 0), (3, 5), (2, 6), (4,)):
        for b in range(2):
            for a in range(2):
                for k in group:
                    owner = ((z - k) % 8) * 4 + (yl ^ a) * 2 + (c ^ b)
                    owners.append(owner)
                    frames += [owner * 2, owner * 2 + 1]
    mine = lax.dynamic_slice(band.reshape(3, 4), (0, kind + 2 * c), (3, 1)).reshape(3)
    result = attend(join(*outs), mine, jnp.stack(frames))
    w = jnp.arange(32, dtype=jnp.int32)
    order = jnp.sum(jnp.where(jnp.stack(owners)[None, :] == w[:, None], w[None, :], 0), axis=1)
    back = lax.all_to_all(reorder(result, order), WIDE, 0, 0, tiled=True)
    g = jnp.arange(4, dtype=jnp.int32)
    return spread(back, ((g % 2) ^ yh) * 2 + g // 2)


def solution(mesh):
    own = Mesh(mesh.devices.reshape(SIZES), NAMES)
    tok = P(WIDE, ("yh", "x"), None)
    placed = (tok, P(), P(None, ("yh", "x")), P())
    return jax.shard_map(per_device, mesh=own, in_specs=placed, out_specs=tok, check_vma=False)
```
